256 devices in a mesh: row: 8 (over x, z_lo), col: 32 (over y, z_hi, core).
Axes of the slice: x: 4, y: 4, z: 8 (z_hi: 4, z_lo: 2; z = z_hi * 2 + z_lo), core: 2. Of those that a mesh axis runs over, the one named last changes fastest.
Arguments:
- query_grads: bfloat16 [1024, 28672], P('col', 'row'), may hold values from -6 to 6
- query_inputs: bfloat16 [1024, 8192], P(None, 'col'), may hold values from -6 to 6
- out_basis: bfloat16 [28672, 28672], P('row', 'col'), may hold values from -0.03125 to 0.03125
- in_basis: bfloat16 [8192, 8192], P('col', 'row'), may hold values from -0.0625 to 0.0625
- eig_grid: bfloat16 [28672, 8192], P('col', 'row'), may hold values from 0.0019989014 to 0.19921875
Outputs:
- scaled: bfloat16 [28672, 8192], P('col', 'row')
The draws below stay inside these ranges and needn't reach their ends.
All inputs are finite; a program needn't handle non-finite values.
Results may differ from the reference program's by a relative error of at most 0.0058.
Values may be sent and summed in bfloat16 or wider, within the bound.
A program may use at most 64 MiB of HBM per device.

```python
import math
import jax
import jax.numpy as jnp
from jax import lax

DOUT = 28672
DIN = 8192
TOKENS = 1024


def levels(own_key, shape, shards, least, largest):
    level, own = 1.0, jax.random.fold_in(own_key, 6)
    for dim, parts in shards:
        steps = jnp.exp(jax.random.uniform(jax.random.fold_in(own, dim), (parts,), jnp.float32, least / len(shards), largest / len(shards)))
        level = level * jnp.repeat(steps, shape[dim] // parts).reshape([-1 if axis == dim else 1 for axis in range(len(shape))])
    return level


def bell_draw(own_key, dims, deviation, bound, cuts=(), held_as=jnp.bfloat16):
    level = levels(own_key, dims, cuts, -0.22, 0.18) if cuts else 1.0
    drawn = jax.random.normal(own_key, dims, jnp.float32) * deviation * level
    return jnp.minimum(jnp.maximum(drawn, -bound), bound).astype(held_as)


def setup_inputs(seed: int = 0) -> dict:
    seeds = jax.random.split(jax.random.key(seed), 6)
    query_grads = bell_draw(seeds[0], (TOKENS, DOUT), 1.0, 6.0, ((0, 32), (1, 8)))
    query_inputs = bell_draw(seeds[1], (TOKENS, DIN), 1.0, 6.0, ((1, 32),))
    out_basis = bell_draw(seeds[2], (DOUT, DOUT), DOUT ** -0.5, 0.03125, ((0, 8), (1, 32)))
    in_basis = bell_draw(seeds[3], (DIN, DIN), DIN ** -0.5, 0.0625, ((0, 32), (1, 8)))
    eig_grid = jnp.clip(jnp.exp(math.log(0.19921875) - 4.6018058 * jax.random.uniform(seeds[4], (DOUT, DIN), jnp.float32) ** levels(seeds[4], (DOUT, DIN), ((0, 32), (1, 8)), -0.2, 0.2)), 0.0019989014, 0.19921875).astype(jnp.bfloat16)
    return {"query_grads": query_grads, "query_inputs": query_inputs, "out_basis": out_basis, "in_basis": in_basis, "eig_grid": eig_grid}


damping = 0.01


def rotate(rows, basis, width, block):
    rows_wide = rows.astype(jnp.float32)

    def one_block(index):
        columns = lax.dynamic_slice_in_dim(basis, (index * block).astype(jnp.int32), block, 1)
        return jnp.dot(rows_wide, columns.astype(jnp.float32)).astype(jnp.bfloat16)

    blocks = lax.map(one_block, jnp.arange(width // block, dtype=jnp.int32))
    return jnp.transpose(blocks, (1, 0, 2)).reshape(rows.shape[0], width)


def reference(query_grads, query_inputs, out_basis, in_basis, eig_grid):
    rotated_out = rotate(query_grads, out_basis, DOUT, DOUT // 28 if DOUT % 28 == 0 else DOUT)
    rotated_in = rotate(query_inputs, in_basis, DIN, DIN // 8 if DIN % 8 == 0 else DIN)
    coeffs = jnp.dot(rotated_out.astype(jnp.float32).T, rotated_in.astype(jnp.float32))
    scaled = coeffs / TOKENS / (eig_grid.astype(jnp.float32) + damping)
    return scaled.astype(jnp.bfloat16)
```

```python
import jax
import jax.numpy as jnp
from jax import lax
from jax.experimental import pallas as pl
from jax.experimental.pallas import tpu as pltpu
from jax.sharding import PartitionSpec as P

damping = 0.01
MESH = pl.DeviceIdType.MESH
SLABS = (0, 1, 3, 2)
MAX_COPIES = 160


def kernel(g_in, q_in, bo_in, bi_in, eig_in, out, G, B, QI, IB, RIp, RIf, RZ, JYb, JYf, RY, RI,
           Pb, Pf, RX, SB, SZ, RO, ACC, EIG, OUT, ssem, rsem, lsem):
    f32, bf16 = jnp.float32, jnp.bfloat16
    r, c = lax.axis_index("row"), lax.axis_index("col")
    x, zl = r // 2, r % 2
    y, zh, k = c // 8, (c // 2) % 4, c % 2

    def dev(dx=0, dy=0, dz=0, flip_zl=False, flip_k=False):
        zl_to = 1 - zl if flip_zl else zl
        k_to = 1 - k if flip_k else k
        return ((x + dx) % 4 * 2 + zl_to, (y + dy) % 4 * 8 + (zh + dz) % 4 * 2 + k_to)

    sib = dev(flip_k=True)
    yp, ym, y2 = dev(dy=1), dev(dy=3), dev(dy=2)
    zp, zm, z2 = dev(dz=1), dev(dz=3), dev(dz=2)
    xp, xm, x2 = dev(dx=1), dev(dx=3), dev(dx=2)
    zlp = dev(flip_zl=True)
    partners = (sib, yp, ym, y2, zp, zm, z2, xp, xm, x2, zlp)

    loads = {}

    def load(name, src, dst):
        cp = pltpu.make_async_copy(src, dst, lsem.at[len(loads)])
        cp.start()
        loads[name] = cp

    load("q", q_in.at[:, :, k], QI.at[k])
    load("bi", bi_in, IB.at[k])
    load("g", g_in, G.at[0, 0, k])
    load("bo", bo_in, B)
    load("eig", eig_in, EIG)

    barrier = pltpu.get_barrier_semaphore()
    for p in partners:
        pl.semaphore_signal(barrier, inc=1, device_id=p, device_id_type=MESH)
    pl.semaphore_wait(barrier, len(partners))

    copies = {}

    def send(name, src, dst, to):
        n = len(copies)
        cp = pltpu.make_async_remote_copy(src_ref=src, dst_ref=dst, send_sem=ssem.at[n], recv_sem=rsem.at[n],
                                          device_id=to, device_id_type=MESH)
        cp.start()
        copies[name] = cp

    def got(name):
        copies[name].wait_recv()

    def gather_z(tag, buf, own):
        send(tag + "z3", own, buf.at[3, 0, k], zp)
        send(tag + "z1", own, buf.at[1, 0, k], zm)

    def gather_y(tag, buf, dz, own):
        send(tag + f"y3{dz}", own, buf.at[dz, 3, k], yp)
        send(tag + f"y1{dz}", own, buf.at[dz, 1, k], ym)
        send(tag + f"s0{dz}", own, buf.at[dz, 0, k], sib)

    lo, hi = pl.ds(0, 16), pl.ds(16, 16)

    def gather_z_arrive(tag, buf):
        got(tag + "z3")
        send(tag + "z2lo", buf.at[3, 0, k, lo], buf.at[2, 0, k, lo], zp)
        gather_y(tag, buf, 3, buf.at[3, 0, k])
        got(tag + "z1")
        send(tag + "z2hi", buf.at[1, 0, k, hi], buf.at[2, 0, k, hi], zm)
        gather_y(tag, buf, 1, buf.at[1, 0, k])

    def gather_z_arrive2(tag, buf):
        got(tag + "z2lo")
        got(tag + "z2hi")
        gather_y(tag, buf, 2, buf.at[2, 0, k])

    def gather_y_arrive(tag, buf, dz):
        got(tag + f"y3{dz}")
        send(tag + f"y2lo{dz}", buf.at[dz, 3, k, lo], buf.at[dz, 2, k, lo], yp)
        send(tag + f"s3{dz}", buf.at[dz, 3, k], buf.at[dz, 3, k], sib)
        got(tag + f"y1{dz}")
        send(tag + f"y2hi{dz}", buf.at[dz, 1, k, hi], buf.at[dz, 1 + 1, k, hi], ym)
        send(tag + f"s1{dz}", buf.at[dz, 1, k], buf.at[dz, 1, k], sib)

    def gather_y_arrive2(tag, buf, dz):
        got(tag + f"y2lo{dz}")
        got(tag + f"y2hi{dz}")
        send(tag + f"s2{dz}", buf.at[dz, 2, k], buf.at[dz, 2, k], sib)

    def gather_sib(tag, dz):
        for dy in range(4):
            got(tag + f"s{dy}{dz}")

    def in_start():
        send("bi", bi_in, IB.at[k], sib)
        send("q", q_in.at[:, :, 1 - k], QI.at[k], sib)

    def in_partial():
        loads["q"].wait()
        loads["bi"].wait()
        got("bi")
        got("q")
        for yy in range(4):
            total = jnp.zeros((128, 1024), f32)
            for kf in range(2):
                total += jnp.dot(QI[kf, yy].reshape(128, 256), IB[kf], preferred_element_type=f32)
            total = total.reshape(4, 32, 1024)
            for zz in range(4):
                RIf[zz, yy] = total[zz]
                RIp[zz, yy] = total[zz].astype(bf16)

    def in_z_send():
        send("iz2", RIp.at[(zh + 2) % 4], RZ.at[0], z2)
        send("iz1", RIp.at[(zh + 1) % 4], RZ.at[1], zp)
        send("iz3", RIp.at[(zh + 3) % 4], RZ.at[2], zm)

    def in_y_send():
        for d in "213":
            got("iz" + d)
        total = RIf[zh]
        for i in range(3):
            total += RZ[i].astype(f32)
        JYf[...] = total
        JYb[...] = total.astype(bf16)
        send("iy2", JYb.at[(y + 2) % 4], RY.at[0], y2)
        send("iy1", JYb.at[(y + 1) % 4], RY.at[1], yp)
        send("iy3", JYb.at[(y + 3) % 4], RY.at[2], ym)

    def in_final():
        for d in "213":
            got("iy" + d)
        total = JYf[y]
        for i in range(3):
            total += RY[i].astype(f32)
        RI[0, 0, k] = total.astype(bf16)
        gather_z("r", RI, RI.at[0, 0, k])
        gather_y("r", RI, 0, RI.at[0, 0, k])

    def out_partial(q):
        slab = G.at[q]
        for n0, n1 in ((0, 512), (512, 896)):
            part = jnp.dot(slab[...].reshape(256, 3584), B[:, n0:n1], preferred_element_type=f32)
            part = part.reshape(4, 2, 32, n1 - n0)
            Pf[q, :, :, :, n0:n1] = part
            Pb[q, :, :, :, n0:n1] = part.astype(bf16)
        send(f"x2{q}", Pb.at[q, (x + 2) % 4], RX.at[q, 0], x2)
        send(f"x1{q}", Pb.at[q, (x + 1) % 4], RX.at[q, 1], xp)
        send(f"x3{q}", Pb.at[q, (x + 3) % 4], RX.at[q, 2], xm)

    def out_x(q):
        for d in "213":
            got(f"x{d}{q}")
        total = Pf[q, x]
        for i in range(3):
            total += RX[q, i].astype(f32)
        Pf[q, x] = total
        SB[q] = Pf[q, x, 1 - zl].astype(bf16)
        send(f"zl{q}", SB.at[q], SZ.at[q], zlp)

    def out_zl(q):
        got(f"zl{q}")
        RO[q, x, zl] = (Pf[q, x, zl] + SZ[q].astype(f32)).astype(bf16)
        mine = RO.at[q, x, zl]
        send(f"oz{q}", mine, mine, zlp)
        send(f"op{q}", mine, mine, xp)
        send(f"om{q}", mine, mine, xm)

    def out_gather1(q):
        got(f"oz{q}")
        other = RO.at[q, x, 1 - zl]
        send(f"opz{q}", other, other, xp)
        send(f"omz{q}", other, other, xm)

    def out_gather2(q):
        for name in ("op", "om", "opz", "omz"):
            got(name + str(q))
        left, right = RO.at[q, (x + 3) % 4, 0], RO.at[q, (x + 1) % 4, 1]
        send(f"o2p{q}", left, left, xp)
        send(f"o2m{q}", right, right, xm)

    def coeffs(q, first):
        got(f"o2p{q}")
        got(f"o2m{q}")
        part = lax.dot_general(RO[q].reshape(256, 896), RI[q].reshape(256, 1024), (((0,), (0,)), ((), ())),
                               preferred_element_type=f32)
        if first:
            ACC[...] = part
        else:
            ACC[...] += part

    gather_z("g", G, g_in)
    gather_y("g", G, 0, g_in)
    in_start()
    in_partial()
    loads["g"].wait()
    gather_y_arrive("g", G, 0)
    gather_z_arrive("g", G)
    in_z_send()
    gather_y_arrive2("g", G, 0)
    gather_sib("g", 0)
    loads["bo"].wait()
    out_partial(0)
    gather_z_arrive2("g", G)
    gather_y_arrive("g", G, 1)
    gather_y_arrive("g", G, 3)
    out_x(0)
    gather_y_arrive2("g", G, 1)
    out_zl(0)
    gather_sib("g", 1)
    out_gather1(0)
    out_partial(1)
    out_gather2(0)
    gather_y_arrive("g", G, 2)
    gather_y_arrive2("g", G, 3)
    out_x(1)
    in_y_send()
    gather_sib("g", 3)
    out_zl(1)
    in_final()
    out_partial(3)
    out_gather1(1)
    gather_y_arrive2("g", G, 2)
    out_gather2(1)
    gather_z_arrive("r", RI)
    gather_sib("g", 2)
    out_partial(2)
    out_x(3)
    gather_y_arrive("r", RI, 0)
    gather_z_arrive2("r", RI)
    out_zl(3)
    gather_y_arrive("r", RI, 1)
    gather_y_arrive("r", RI, 3)
    out_x(2)
    out_gather1(3)
    gather_y_arrive("r", RI, 2)
    out_zl(2)
    gather_y_arrive2("r", RI, 0)
    gather_y_arrive2("r", RI, 1)
    out_gather2(3)
    out_gather1(2)
    gather_y_arrive2("r", RI, 3)
    gather_y_arrive2("r", RI, 2)
    gather_sib("r", 0)
    coeffs(0, True)
    out_gather2(2)
    gather_sib("r", 1)
    coeffs(1, False)
    gather_sib("r", 3)
    coeffs(3, False)
    gather_sib("r", 2)
    coeffs(2, False)
    loads["eig"].wait()
    outs = []
    for i in range(4):
        rows = pl.ds(i * 224, 224)
        OUT[rows] = (ACC[rows] / 1024 / (EIG[rows].astype(f32) + damping)).astype(bf16)
        cp = pltpu.make_async_copy(OUT.at[rows], out.at[rows], lsem.at[len(loads) + i])
        cp.start()
        outs.append(cp)
    for cp in copies.values():
        cp.wait_send()
    for cp in outs:
        cp.wait()


def shards(query_grads, query_inputs, out_basis, in_basis, eig_grid):
    bf16, f32, vmem = jnp.bfloat16, jnp.float32, pltpu.VMEM
    any_space = pl.BlockSpec(memory_space=pl.ANY)
    return pl.pallas_call(
        kernel,
        out_shape=jax.ShapeDtypeStruct((896, 1024), bf16),
        in_specs=[any_space] * 5,
        out_specs=any_space,
        scratch_shapes=[
            vmem((4, 4, 2, 32, 3584), bf16),
            vmem((3584, 896), bf16),
            vmem((2, 4, 4, 32, 256), bf16),
            vmem((2, 256, 1024), bf16),
            vmem((4, 4, 32, 1024), bf16),
            vmem((4, 4, 32, 1024), f32),
            vmem((3, 4, 32, 1024), bf16),
            vmem((4, 32, 1024), bf16),
            vmem((4, 32, 1024), f32),
            vmem((3, 32, 1024), bf16),
            vmem((4, 4, 2, 32, 1024), bf16),
            vmem((4, 4, 2, 32, 896), bf16),
            vmem((4, 4, 2, 32, 896), f32),
            vmem((4, 3, 2, 32, 896), bf16),
            vmem((4, 32, 896), bf16),
            vmem((4, 32, 896), bf16),
            vmem((4, 4, 2, 32, 896), bf16),
            vmem((896, 1024), f32),
            vmem((896, 1024), bf16),
            vmem((896, 1024), bf16),
            pltpu.SemaphoreType.DMA((MAX_COPIES,)),
            pltpu.SemaphoreType.DMA((MAX_COPIES,)),
            pltpu.SemaphoreType.DMA((9,)),
        ],
        compiler_params=pltpu.CompilerParams(
            collective_id=0, has_side_effects=True, vmem_limit_bytes=56 * 2**20
        ),
        cost_estimate=pl.CostEstimate(flops=9_000_000_000, bytes_accessed=12_000_000, transcendentals=0),
        name="precondition",
    )(query_grads, query_inputs.reshape(4, 4, 2, 32, 256), out_basis, in_basis, eig_grid)


def solution(mesh):
    return jax.shard_map(
        shards,
        mesh=mesh,
        in_specs=(
            P("col", "row"),
            P(None, "col"),
            P("row", "col"),
            P("col", "row"),
            P("col", "row"),
        ),
        out_specs=P("col", "row"),
        check_vma=False,
    )
```

```python
import jax
import jax.numpy as jnp
from jax import lax
from jax.experimental import pallas as pl
from jax.experimental.pallas import tpu as pltpu
from jax.sharding import PartitionSpec as P

damping = 0.01
MESH = pl.DeviceIdType.MESH
SENT, ARRIVED = 12, 101


def kernel(g_in, q_in, bo_in, bi_in, eig_in, out, G, B, QI, IB, RIp, RIf, RZ, JYb, JYf, RY, RI,
           Pb, Pf, RX, SB, SZ, RO, ACC, EIG, OUT, ssem, rsem, lsem):
    f32, bf16 = jnp.float32, jnp.bfloat16
    r, c = lax.axis_index("row"), lax.axis_index("col")
    x, zl = r // 2, r % 2
    y, zh, k = c // 8, (c // 2) % 4, c % 2

    def dev(dx=0, dy=0, dz=0, flip_zl=False, flip_k=False):
        zl_to = 1 - zl if flip_zl else zl
        k_to = 1 - k if flip_k else k
        return ((x + dx) % 4 * 2 + zl_to, (y + dy) % 4 * 8 + (zh + dz) % 4 * 2 + k_to)

    sib = dev(flip_k=True)
    yp, ym, y2 = dev(dy=1), dev(dy=3), dev(dy=2)
    zp, zm, z2 = dev(dz=1), dev(dz=3), dev(dz=2)
    xp, xm, x2 = dev(dx=1), dev(dx=3), dev(dx=2)
    zlp = dev(flip_zl=True)
    partners = (sib, yp, ym, y2, zp, zm, z2, xp, xm, x2, zlp)

    loads = {}

    def load(name, src, dst):
        cp = pltpu.make_async_copy(src, dst, lsem.at[len(loads)])
        cp.start()
        loads[name] = cp

    load("q", q_in.at[:, :, k], QI.at[k])
    load("bi", bi_in, IB.at[k])
    load("g", g_in, G.at[0, 0, k])
    load("bo", bo_in, B)
    load("eig", eig_in, EIG)

    barrier = pltpu.get_barrier_semaphore()
    for p in partners:
        pl.semaphore_signal(barrier, inc=1, device_id=p, device_id_type=MESH)
    pl.semaphore_wait(barrier, len(partners))

    sent, arrived = {}, {}

    def copy(group, name, src, dst, to):
        out_sem = ssem.at[sent.setdefault(group, len(sent))]
        in_sem = rsem.at[arrived.setdefault(name, len(arrived))]
        return pltpu.make_async_remote_copy(src_ref=src, dst_ref=dst, send_sem=out_sem, recv_sem=in_sem,
                                            device_id=to, device_id_type=MESH)

    def send(group, name, src, dst, to):
        copy(group, name, src, dst, to).start()

    def got(name, ref):
        copy("ibi", name, ref, ref, sib).wait_recv()

    def all_sent(group, ref):
        copy(group, "ibi", ref, ref, sib).wait_send()

    def part(buf, q, h, dy):
        return buf.at[q, dy, k, pl.ds(16 * h, 16)]

    def send_y(t, buf, q, halves):
        for h in (0, 1):
            send(t + "y", f"{t}y3{q}{h}", halves[h], part(buf, q, h, 3), yp)
            send(t + "y", f"{t}y1{q}{1 - h}", halves[1 - h], part(buf, q, 1 - h, 1), ym)

    def gather_start(t, buf, own):
        halves = [own.at[pl.ds(16 * h, 16)] for h in range(2)]
        send(t + "z", t + "z1", halves[0], part(buf, 1, 0, 0), zp)
        send(t + "z", t + "z1", halves[1], part(buf, 1, 1, 0), zm)
        send(t + "z", t + "z2", halves[1], part(buf, 2, 1, 0), zp)
        send(t + "z", t + "z2", halves[0], part(buf, 2, 0, 0), zm)
        send_y(t, buf, 0, halves)
        send(t + "s", t + "s0", own, buf.at[0, 0, k], sib)

    def gather_z(t, buf, q):
        got(f"{t}z{q}", buf.at[q, 0, k])
        halves = [part(buf, q, h, 0) for h in range(2)]
        if q == 1:
            send(t + "z", t + "z3", halves[0], part(buf, 3, 0, 0), zp)
            send(t + "z", t + "z3", halves[1], part(buf, 3, 1, 0), zm)
        send_y(t, buf, q, halves)
        send(t + "s", f"{t}s{q}", buf.at[q, 0, k], buf.at[q, 0, k], sib)

    def gather_y(t, buf, dy, q, h):
        src = part(buf, q, h, dy)
        got(f"{t}y{dy}{q}{h}", src)
        if (dy, h) == (3, 0):
            send(t + "y", f"{t}y2{q}", src, part(buf, q, 0, 2), yp)
        if (dy, h) == (1, 1):
            send(t + "y", f"{t}y2{q}", src, part(buf, q, 1, 2), ym)
        send(t + "s", f"{t}s{q}", src, src, sib)

    def gather_far(t, buf, q):
        src = buf.at[q, 2, k]
        got(f"{t}y2{q}", src)
        send(t + "s", f"{t}s{q}", src, src, sib)

    def gather_done(t, buf, q):
        got(f"{t}s{q}", buf.at[q, :, 1 - k])

    def in_start():
        send("ibi", "ibi", bi_in, IB.at[k], sib)
        send("iq", "iq", q_in.at[:, :, 1 - k], QI.at[k], sib)

    def in_partial():
        loads["q"].wait()
        loads["bi"].wait()
        got("ibi", IB.at[1 - k])
        got("iq", QI.at[1 - k])
        for yy in range(4):
            total = jnp.zeros((128, 1024), f32)
            for kf in range(2):
                total += jnp.dot(QI[kf, yy].reshape(128, 256), IB[kf], preferred_element_type=f32)
            total = total.reshape(4, 32, 1024)
            for zz in range(4):
                RIf[zz, yy] = total[zz]
                RIp[zz, yy] = total[zz].astype(bf16)

    zn, zb, zo = (zh + 1) % 4, (zh + 3) % 4, (zh + 2) % 4
    lo, hi = pl.ds(0, 16), pl.ds(16, 16)

    def in_far(j):
        yj = (y + j) % 4
        send("i", f"iA+{j}", RIp.at[zo, yj, lo], RZ.at[0, j], zp)
        send("i", f"iA-{j}", RIp.at[zo, yj, hi], RZ.at[1, j], zm)

    def in_near(j):
        yj = (y + j) % 4
        send("i", f"iD{j}", RIp.at[zn, yj, hi], RZ.at[2, j], zp)
        send("i", f"iD{j}", RIp.at[zb, yj, lo], RZ.at[3, j], zm)

    def in_add(way, j):
        got(f"iA{way}{j}", RZ.at[0 if way == "+" else 1, j])
        yj = (y + j) % 4
        if way == "+":
            RIp[zn, yj, lo] = (RIf[zn, yj, lo] + RZ[0, j].astype(f32)).astype(bf16)
            send("i", f"iD{j}", RIp.at[zn, yj, lo], RZ.at[4, j], zp)
        else:
            RIp[zb, yj, hi] = (RIf[zb, yj, hi] + RZ[1, j].astype(f32)).astype(bf16)
            send("i", f"iD{j}", RIp.at[zb, yj, hi], RZ.at[5, j], zm)

    def in_y(j):
        got(f"iD{j}", RZ.at[pl.ds(2, 4), j])
        yj = (y + j) % 4
        first = RIf[zh, yj, lo] + RZ[4, j].astype(f32) + RZ[3, j].astype(f32)
        second = RIf[zh, yj, hi] + RZ[2, j].astype(f32) + RZ[5, j].astype(f32)
        if j == 0:
            JYf[lo] = first
            JYf[hi] = second
        else:
            JYb[j, lo] = first.astype(bf16)
            JYb[j, hi] = second.astype(bf16)
            send("iy", "iy", JYb.at[j], RY.at[j - 1], (yp, y2, ym)[j - 1])

    def in_final():
        got("iy", RY)
        total = JYf[...]
        for i in range(3):
            total += RY[i].astype(f32)
        RI[0, 0, k] = total.astype(bf16)

    xn, xb, xo = (x + 1) % 4, (x + 3) % 4, (x + 2) % 4

    def out_partial(q, n):
        n0, n1 = ((0, 512), (512, 896))[n]
        total = jnp.dot(G[q].reshape(256, 3584), B[:, n0:n1], preferred_element_type=f32)
        total = total.reshape(4, 2, 32, n1 - n0)
        Pf[q, :, :, :, n0:n1] = total
        Pb[q, :, :, :, n0:n1] = total.astype(bf16)
        if n == 1:
            send("x", f"A+{q}", Pb.at[q, xo, 0], RX.at[q, 0], xp)
            send("x", f"A-{q}", Pb.at[q, xo, 1], RX.at[q, 1], xm)
            send("x", f"D{q}", Pb.at[q, xn, 1], RX.at[q, 2], xp)
            send("x", f"D{q}", Pb.at[q, xb, 0], RX.at[q, 3], xm)

    def out_add(way, q):
        got(f"A{way}{q}", RX.at[q, 0 if way == "+" else 1])
        if way == "+":
            Pb[q, xn, 0] = (Pf[q, xn, 0] + RX[q, 0].astype(f32)).astype(bf16)
            send("x", f"D{q}", Pb.at[q, xn, 0], RX.at[q, 4], xp)
        else:
            Pb[q, xb, 1] = (Pf[q, xb, 1] + RX[q, 1].astype(f32)).astype(bf16)
            send("x", f"D{q}", Pb.at[q, xb, 1], RX.at[q, 5], xm)

    def out_x(q):
        got(f"D{q}", RX.at[q, pl.ds(2, 4)])
        Pf[q, x, 0] = Pf[q, x, 0] + RX[q, 4].astype(f32) + RX[q, 3].astype(f32)
        Pf[q, x, 1] = Pf[q, x, 1] + RX[q, 2].astype(f32) + RX[q, 5].astype(f32)
        SB[q] = Pf[q, x, 1 - zl].astype(bf16)
        send("o", f"zl{q}", SB.at[q], SZ.at[q], zlp)

    def out_zl(q):
        got(f"zl{q}", SZ.at[q])
        RO[q, x, zl] = (Pf[q, x, zl] + SZ[q].astype(f32)).astype(bf16)
        mine = RO.at[q, x, zl]
        send("o", f"oz{q}", mine, mine, zlp)
        send("o", f"op{q}", mine, mine, xp)
        send("o", f"o{q}", mine, mine, xm)

    def out_pair(q):
        other = RO.at[q, x, 1 - zl]
        got(f"oz{q}", other)
        send("o", f"o{q}", other, other, xp)
        send("o", f"omz{q}", other, other, xm)

    def out_far(way, q):
        if way == "+":
            src = RO.at[q, xb, zl]
            got(f"op{q}", src)
            send("o", f"o{q}", src, src, xp)
        else:
            src = RO.at[q, xn, 1 - zl]
            got(f"omz{q}", src)
            send("o", f"o{q}", src, src, xm)

    def rotated(q):
        got(f"o{q}", RO.at[q, pl.ds(0, 2)])
        gather_done("r", RI, q)

    def product(left, right):
        return lax.dot_general(left, right, (((0,), (0,)), ((), ())), preferred_element_type=f32)

    outs = []

    def coeffs(q):
        if q == 0:
            rotated(0)
            rotated(1)
            ACC[...] = product(RO[0:2].reshape(512, 896), RI[0:2].reshape(512, 1024))
        elif q == 2:
            rotated(2)
            ACC[...] += product(RO[2].reshape(256, 896), RI[2].reshape(256, 1024))
        else:
            rotated(3)
            loads["eig"].wait()
            right = RI[3].reshape(256, 1024)
            for i, (m, n) in enumerate(((0, 256), (256, 512), (512, 768), (768, 896))):
                total = ACC[m:n] + product(RO[3, :, :, :, m:n].reshape(256, n - m), right)
                OUT[m:n] = (total / 1024 / (EIG[m:n].astype(f32) + damping)).astype(bf16)
                cp = pltpu.make_async_copy(OUT.at[pl.ds(m, n - m)], out.at[pl.ds(m, n - m)], lsem.at[len(loads) + i])
                cp.start()
                outs.append(cp)

    def drain():
        for t, buf in (("g", G), ("r", RI)):
            all_sent(t + "z", buf.at[pl.ds(0, 3), 0, 0])
            all_sent(t + "y", buf.at[pl.ds(0, 3), :, 0])
            all_sent(t + "s", buf.at[pl.ds(0, 2)])
        for group, ref in (("ibi", IB.at[k]), ("iq", QI.at[k]), ("i", RZ), ("iy", RY), ("x", RX), ("o", RO)):
            all_sent(group, ref)
        for cp in outs:
            cp.wait()

    gather_start("g", G, g_in)
    in_start()
    in_partial()
    gather_y("g", G, 3, 0, 0)
    gather_y("g", G, 1, 0, 1)
    gather_y("g", G, 1, 0, 0)
    gather_y("g", G, 3, 0, 1)
    in_near(0)
    gather_z("g", G, 1)
    gather_far("g", G, 0)
    loads["g"].wait()
    loads["bo"].wait()
    gather_done("g", G, 0)
    out_partial(0, 0)
    gather_y("g", G, 3, 1, 0)
    gather_y("g", G, 1, 1, 1)
    out_partial(0, 1)
    gather_z("g", G, 2)
    in_far(0)
    in_far(1)
    gather_y("g", G, 1, 1, 0)
    gather_y("g", G, 3, 1, 1)
    in_far(2)
    out_add("+", 0)
    out_add("-", 0)
    gather_far("g", G, 1)
    in_far(3)
    in_near(1)
    gather_done("g", G, 1)
    out_partial(1, 0)
    gather_y("g", G, 3, 2, 0)
    gather_y("g", G, 1, 2, 1)
    in_add("+", 0)
    in_add("-", 0)
    gather_z("g", G, 3)
    out_x(0)
    out_partial(1, 1)
    gather_y("g", G, 1, 2, 0)
    gather_y("g", G, 3, 2, 1)
    in_add("+", 1)
    in_add("-", 1)
    in_add("+", 2)
    in_add("-", 2)
    in_add("+", 3)
    gather_far("g", G, 2)
    in_add("-", 3)
    out_add("+", 1)
    out_add("-", 1)
    in_near(2)
    gather_done("g", G, 2)
    out_partial(2, 0)
    in_y(0)
    gather_y("g", G, 3, 3, 0)
    gather_y("g", G, 1, 3, 1)
    in_near(3)
    out_zl(0)
    out_x(1)
    out_partial(2, 1)
    gather_y("g", G, 1, 3, 0)
    gather_y("g", G, 3, 3, 1)
    in_y(1)
    out_far("+", 0)
    gather_far("g", G, 3)
    out_add("+", 2)
    out_add("-", 2)
    in_y(2)
    gather_done("g", G, 3)
    out_partial(3, 0)
    in_y(3)
    out_pair(0)
    out_partial(3, 1)
    out_zl(1)
    out_x(2)
    out_far("-", 0)
    in_final()
    gather_start("r", RI, RI.at[0, 0, k])
    out_add("+", 3)
    out_pair(1)
    out_add("-", 3)
    out_zl(2)
    gather_y("r", RI, 1, 0, 1)
    gather_y("r", RI, 3, 0, 0)
    gather_y("r", RI, 1, 0, 0)
    gather_y("r", RI, 3, 0, 1)
    out_far("+", 1)
    gather_z("r", RI, 1)
    gather_far("r", RI, 0)
    out_far("-", 1)
    out_pair(2)
    gather_z("r", RI, 2)
    gather_y("r", RI, 1, 1, 1)
    gather_y("r", RI, 3, 1, 0)
    out_far("+", 2)
    out_x(3)
    gather_y("r", RI, 1, 1, 0)
    gather_y("r", RI, 3, 1, 1)
    gather_y("r", RI, 1, 2, 1)
    gather_y("r", RI, 3, 2, 0)
    gather_z("r", RI, 3)
    gather_y("r", RI, 1, 2, 0)
    gather_y("r", RI, 3, 2, 1)
    gather_far("r", RI, 1)
    out_zl(3)
    out_far("-", 2)
    gather_far("r", RI, 2)
    gather_y("r", RI, 1, 3, 1)
    gather_y("r", RI, 3, 3, 0)
    coeffs(0)
    gather_y("r", RI, 1, 3, 0)
    gather_y("r", RI, 3, 3, 1)
    out_pair(3)
    out_far("+", 3)
    gather_far("r", RI, 3)
    coeffs(2)
    out_far("-", 3)
    coeffs(3)
    drain()
    assert (len(sent), len(arrived)) == (SENT, ARRIVED), (len(sent), len(arrived))


def shards(query_grads, query_inputs, out_basis, in_basis, eig_grid):
    bf16, f32, vmem = jnp.bfloat16, jnp.float32, pltpu.VMEM
    any_space = pl.BlockSpec(memory_space=pl.ANY)
    return pl.pallas_call(
        kernel,
        out_shape=jax.ShapeDtypeStruct((896, 1024), bf16),
        in_specs=[any_space] * 5,
        out_specs=any_space,
        scratch_shapes=[
            vmem((4, 4, 2, 32, 3584), bf16),
            vmem((3584, 896), bf16),
            vmem((2, 4, 4, 32, 256), bf16),
            vmem((2, 256, 1024), bf16),
            vmem((4, 4, 32, 1024), bf16),
            vmem((4, 4, 32, 1024), f32),
            vmem((6, 4, 16, 1024), bf16),
            vmem((4, 32, 1024), bf16),
            vmem((32, 1024), f32),
            vmem((3, 32, 1024), bf16),
            vmem((4, 4, 2, 32, 1024), bf16),
            vmem((4, 4, 2, 32, 896), bf16),
            vmem((4, 4, 2, 32, 896), f32),
            vmem((4, 6, 32, 896), bf16),
            vmem((4, 32, 896), bf16),
            vmem((4, 32, 896), bf16),
            vmem((4, 4, 2, 32, 896), bf16),
            vmem((896, 1024), f32),
            vmem((896, 1024), bf16),
            vmem((896, 1024), bf16),
            pltpu.SemaphoreType.DMA((SENT,)),
            pltpu.SemaphoreType.DMA((ARRIVED,)),
            pltpu.SemaphoreType.DMA((9,)),
        ],
        compiler_params=pltpu.CompilerParams(
            collective_id=0, has_side_effects=True, vmem_limit_bytes=56 * 2**20
        ),
        cost_estimate=pl.CostEstimate(flops=9_000_000_000, bytes_accessed=12_000_000, transcendentals=0),
        name="precondition",
    )(query_grads, query_inputs.reshape(4, 4, 2, 32, 256), out_basis, in_basis, eig_grid)


def solution(mesh):
    return jax.shard_map(
        shards,
        mesh=mesh,
        in_specs=(
            P("col", "row"),
            P(None, "col"),
            P("row", "col"),
            P("col", "row"),
            P("col", "row"),
        ),
        out_specs=P("col", "row"),
        check_vma=False,
    )
```

```python
import jax
import jax.numpy as jnp
from jax import lax
from jax.experimental import pallas as pl
from jax.experimental.pallas import tpu as pltpu
from jax.sharding import PartitionSpec as P

damping = 0.01
MESH = pl.DeviceIdType.MESH
SENT, ARRIVED = 12, 101


def kernel(g_in, q_in, bo_in, bi_in, eig_in, out, G, B, QI, IB, RIp, RIf, RZ, JYb, JYf, RY, RI,
           Pb, Pf, RX, SB, SZ, RO, ACC, EIG, OUT, ssem, rsem, lsem):
    f32, bf16 = jnp.float32, jnp.bfloat16
    r, c = lax.axis_index("row"), lax.axis_index("col")
    x, zl = r // 2, r % 2
    y, zh, k = c // 8, (c // 2) % 4, c % 2

    def dev(dx=0, dy=0, dz=0, flip_zl=False, flip_k=False):
        zl_to = 1 - zl if flip_zl else zl
        k_to = 1 - k if flip_k else k
        return ((x + dx) % 4 * 2 + zl_to, (y + dy) % 4 * 8 + (zh + dz) % 4 * 2 + k_to)

    sib = dev(flip_k=True)
    yp, ym, y2 = dev(dy=1), dev(dy=3), dev(dy=2)
    zp, zm, z2 = dev(dz=1), dev(dz=3), dev(dz=2)
    xp, xm, x2 = dev(dx=1), dev(dx=3), dev(dx=2)
    zlp = dev(flip_zl=True)
    partners = (sib, yp, ym, y2, zp, zm, z2, xp, xm, x2, zlp)

    loads = {}

    def load(name, src, dst):
        cp = pltpu.make_async_copy(src, dst, lsem.at[len(loads)])
        cp.start()
        loads[name] = cp

    load("q", q_in.at[:, :, k], QI.at[k])
    load("bi", bi_in, IB.at[k])
    load("g", g_in, G.at[0, 0, k])
    load("bo", bo_in, B)
    load("eig", eig_in, EIG)

    barrier = pltpu.get_barrier_semaphore()
    for p in partners:
        pl.semaphore_signal(barrier, inc=1, device_id=p, device_id_type=MESH)
    pl.semaphore_wait(barrier, len(partners))

    sent, arrived = {}, {}

    def copy(group, name, src, dst, to):
        out_sem = ssem.at[sent.setdefault(group, len(sent))]
        in_sem = rsem.at[arrived.setdefault(name, len(arrived))]
        return pltpu.make_async_remote_copy(src_ref=src, dst_ref=dst, send_sem=out_sem, recv_sem=in_sem,
                                            device_id=to, device_id_type=MESH)

    def send(group, name, src, dst, to):
        copy(group, name, src, dst, to).start()

    def got(name, ref):
        copy("ibi", name, ref, ref, sib).wait_recv()

    def all_sent(group, ref):
        copy(group, "ibi", ref, ref, sib).wait_send()

    def part(buf, q, h, dy):
        return buf.at[q, dy, k, pl.ds(16 * h, 16)]

    def send_y(t, buf, q, halves):
        for h in (0, 1):
            send(t + "y", f"{t}y3{q}{h}", halves[h], part(buf, q, h, 3), yp)
            send(t + "y", f"{t}y1{q}{1 - h}", halves[1 - h], part(buf, q, 1 - h, 1), ym)

    def gather_start(t, buf, own):
        halves = [own.at[pl.ds(16 * h, 16)] for h in range(2)]
        send(t + "z", t + "z1", halves[0], part(buf, 1, 0, 0), zp)
        send(t + "z", t + "z1", halves[1], part(buf, 1, 1, 0), zm)
        send(t + "z", t + "z2", halves[1], part(buf, 2, 1, 0), zp)
        send(t + "z", t + "z2", halves[0], part(buf, 2, 0, 0), zm)
        send_y(t, buf, 0, halves)
        send(t + "s", t + "s0", own, buf.at[0, 0, k], sib)

    def gather_z(t, buf, q):
        got(f"{t}z{q}", buf.at[q, 0, k])
        halves = [part(buf, q, h, 0) for h in range(2)]
        if q == 1:
            send(t + "z", t + "z3", halves[0], part(buf, 3, 0, 0), zp)
            send(t + "z", t + "z3", halves[1], part(buf, 3, 1, 0), zm)
        send_y(t, buf, q, halves)
        send(t + "s", f"{t}s{q}", buf.at[q, 0, k], buf.at[q, 0, k], sib)

    def gather_y(t, buf, dy, q, h):
        src = part(buf, q, h, dy)
        got(f"{t}y{dy}{q}{h}", src)
        if (dy, h) == (3, 0):
            send(t + "y", f"{t}y2{q}", src, part(buf, q, 0, 2), yp)
        if (dy, h) == (1, 1):
            send(t + "y", f"{t}y2{q}", src, part(buf, q, 1, 2), ym)
        send(t + "s", f"{t}s{q}", src, src, sib)

    def gather_far(t, buf, q):
        src = buf.at[q, 2, k]
        got(f"{t}y2{q}", src)
        send(t + "s", f"{t}s{q}", src, src, sib)

    def gather_done(t, buf, q):
        got(f"{t}s{q}", buf.at[q, :, 1 - k])

    def in_start():
        send("ibi", "ibi", bi_in, IB.at[k], sib)
        send("iq", "iq", q_in.at[:, :, 1 - k], QI.at[k], sib)

    def in_partial():
        loads["q"].wait()
        loads["bi"].wait()
        got("ibi", IB.at[1 - k])
        got("iq", QI.at[1 - k])
        for yy in range(4):
            total = jnp.zeros((128, 1024), f32)
            for kf in range(2):
                total += jnp.dot(QI[kf, yy].reshape(128, 256), IB[kf], preferred_element_type=f32)
            total = total.reshape(4, 32, 1024)
            for zz in range(4):
                RIf[zz, yy] = total[zz]
                RIp[zz, yy] = total[zz].astype(bf16)

    zn, zb, zo = (zh + 1) % 4, (zh + 3) % 4, (zh + 2) % 4
    lo, hi = pl.ds(0, 16), pl.ds(16, 16)

    def in_far(j):
        yj = (y + j) % 4
        send("i", f"iA+{j}", RIp.at[zo, yj, lo], RZ.at[0, j], zp)
        send("i", f"iA-{j}", RIp.at[zo, yj, hi], RZ.at[1, j], zm)

    def in_near(j):
        yj = (y + j) % 4
        send("i", f"iD{j}", RIp.at[zn, yj, hi], RZ.at[2, j], zp)
        send("i", f"iD{j}", RIp.at[zb, yj, lo], RZ.at[3, j], zm)

    def in_add(way, j):
        got(f"iA{way}{j}", RZ.at[0 if way == "+" else 1, j])
        yj = (y + j) % 4
        if way == "+":
            RIp[zn, yj, lo] = (RIf[zn, yj, lo] + RZ[0, j].astype(f32)).astype(bf16)
            send("i", f"iD{j}", RIp.at[zn, yj, lo], RZ.at[4, j], zp)
        else:
            RIp[zb, yj, hi] = (RIf[zb, yj, hi] + RZ[1, j].astype(f32)).astype(bf16)
            send("i", f"iD{j}", RIp.at[zb, yj, hi], RZ.at[5, j], zm)

    def in_y(j):
        got(f"iD{j}", RZ.at[pl.ds(2, 4), j])
        yj = (y + j) % 4
        first = RIf[zh, yj, lo] + RZ[4, j].astype(f32) + RZ[3, j].astype(f32)
        second = RIf[zh, yj, hi] + RZ[2, j].astype(f32) + RZ[5, j].astype(f32)
        if j == 0:
            JYf[lo] = first
            JYf[hi] = second
        else:
            JYb[j, lo] = first.astype(bf16)
            JYb[j, hi] = second.astype(bf16)
            send("iy", "iy", JYb.at[j], RY.at[j - 1], (yp, y2, ym)[j - 1])

    def in_final():
        got("iy", RY)
        total = JYf[...]
        for i in range(3):
            total += RY[i].astype(f32)
        RI[0, 0, k] = total.astype(bf16)

    xn, xb, xo = (x + 1) % 4, (x + 3) % 4, (x + 2) % 4

    def out_partial(q, n):
        n0, n1 = ((0, 512), (512, 896))[n]
        total = jnp.dot(G[q].reshape(256, 3584), B[:, n0:n1], preferred_element_type=f32)
        total = total.reshape(4, 2, 32, n1 - n0)
        Pf[q, :, :, :, n0:n1] = total
        Pb[q, :, :, :, n0:n1] = total.astype(bf16)
        if n == 1:
            send("x", f"A+{q}", Pb.at[q, xo, 0], RX.at[q, 0], xp)
            send("x", f"A-{q}", Pb.at[q, xo, 1], RX.at[q, 1], xm)
            send("x", f"D{q}", Pb.at[q, xn, 1], RX.at[q, 2], xp)
            send("x", f"D{q}", Pb.at[q, xb, 0], RX.at[q, 3], xm)

    def out_add(way, q):
        got(f"A{way}{q}", RX.at[q, 0 if way == "+" else 1])
        if way == "+":
            Pb[q, xn, 0] = (Pf[q, xn, 0] + RX[q, 0].astype(f32)).astype(bf16)
            send("x", f"D{q}", Pb.at[q, xn, 0], RX.at[q, 4], xp)
        else:
            Pb[q, xb, 1] = (Pf[q, xb, 1] + RX[q, 1].astype(f32)).astype(bf16)
            send("x", f"D{q}", Pb.at[q, xb, 1], RX.at[q, 5], xm)

    def out_x(q):
        got(f"D{q}", RX.at[q, pl.ds(2, 4)])
        Pf[q, x, 0] = Pf[q, x, 0] + RX[q, 4].astype(f32) + RX[q, 3].astype(f32)
        Pf[q, x, 1] = Pf[q, x, 1] + RX[q, 2].astype(f32) + RX[q, 5].astype(f32)
        SB[q] = Pf[q, x, 1 - zl].astype(bf16)
        send("o", f"zl{q}", SB.at[q], SZ.at[q], zlp)

    def out_zl(q):
        got(f"zl{q}", SZ.at[q])
        RO[q, x, zl] = (Pf[q, x, zl] + SZ[q].astype(f32)).astype(bf16)
        mine = RO.at[q, x, zl]
        send("o", f"oz{q}", mine, mine, zlp)
        send("o", f"op{q}", mine, mine, xp)
        send("o", f"o{q}", mine, mine, xm)

    def out_pair(q):
        other = RO.at[q, x, 1 - zl]
        got(f"oz{q}", other)
        send("o", f"o{q}", other, other, xp)
        send("o", f"omz{q}", other, other, xm)

    def out_far(way, q):
        if way == "+":
            src = RO.at[q, xb, zl]
            got(f"op{q}", src)
            send("o", f"o{q}", src, src, xp)
        else:
            src = RO.at[q, xn, 1 - zl]
            got(f"omz{q}", src)
            send("o", f"o{q}", src, src, xm)

    def rotated(q):
        got(f"o{q}", RO.at[q, pl.ds(0, 2)])
        gather_done("r", RI, q)

    def product(left, right):
        return lax.dot_general(left, right, (((0,), (0,)), ((), ())), preferred_element_type=f32)

    outs = []

    def coeffs(q):
        if q == 0:
            rotated(0)
            rotated(1)
            ACC[...] = product(RO[0:2].reshape(512, 896), RI[0:2].reshape(512, 1024))
        elif q == 2:
            rotated(2)
            ACC[...] += product(RO[2].reshape(256, 896), RI[2].reshape(256, 1024))
        else:
            rotated(3)
            loads["eig"].wait()
            right = RI[3].reshape(256, 1024)
            for i, (m, n) in enumerate(((0, 256), (256, 512), (512, 768), (768, 896))):
                total = ACC[m:n] + product(RO[3, :, :, :, m:n].reshape(256, n - m), right)
                OUT[m:n] = (total / 1024 / (EIG[m:n].astype(f32) + damping)).astype(bf16)
                cp = pltpu.make_async_copy(OUT.at[pl.ds(m, n - m)], out.at[pl.ds(m, n - m)], lsem.at[len(loads) + i])
                cp.start()
                outs.append(cp)

    def drain():
        for t, buf in (("g", G), ("r", RI)):
            all_sent(t + "z", buf.at[pl.ds(0, 3), 0, 0])
            all_sent(t + "y", buf.at[pl.ds(0, 3), :, 0])
            all_sent(t + "s", buf.at[pl.ds(0, 2)])
        for group, ref in (("ibi", IB.at[k]), ("iq", QI.at[k]), ("i", RZ), ("iy", RY), ("x", RX), ("o", RO)):
            all_sent(group, ref)
        for cp in outs:
            cp.wait()

    gather_start("g", G, g_in)
    in_start()
    in_partial()
    gather_y("g", G, 3, 0, 0)
    gather_y("g", G, 1, 0, 1)
    gather_y("g", G, 1, 0, 0)
    gather_y("g", G, 3, 0, 1)
    in_near(0)
    gather_z("g", G, 1)
    gather_far("g", G, 0)
    loads["g"].wait()
    loads["bo"].wait()
    gather_done("g", G, 0)
    out_partial(0, 0)
    gather_y("g", G, 3, 1, 0)
    gather_y("g", G, 1, 1, 1)
    out_partial(0, 1)
    gather_z("g", G, 2)
    in_far(0)
    in_far(1)
    gather_y("g", G, 1, 1, 0)
    gather_y("g", G, 3, 1, 1)
    in_far(2)
    out_add("+", 0)
    out_add("-", 0)
    gather_far("g", G, 1)
    in_far(3)
    in_near(1)
    gather_y("g", G, 3, 2, 0)
    gather_y("g", G, 1, 2, 1)
    gather_done("g", G, 1)
    out_partial(1, 0)
    in_add("+", 0)
    in_add("-", 0)
    gather_z("g", G, 3)
    out_x(0)
    out_partial(1, 1)
    gather_y("g", G, 1, 2, 0)
    gather_y("g", G, 3, 2, 1)
    in_add("+", 1)
    in_add("-", 1)
    in_add("+", 2)
    in_add("-", 2)
    in_add("+", 3)
    gather_far("g", G, 2)
    in_add("-", 3)
    out_add("+", 1)
    out_add("-", 1)
    in_near(2)
    in_near(3)
    gather_y("g", G, 3, 3, 0)
    gather_y("g", G, 1, 3, 1)
    gather_done("g", G, 2)
    out_partial(2, 0)
    in_y(0)
    out_zl(0)
    out_x(1)
    out_partial(2, 1)
    gather_y("g", G, 1, 3, 0)
    gather_y("g", G, 3, 3, 1)
    in_y(1)
    out_far("+", 0)
    out_pair(0)
    gather_far("g", G, 3)
    out_add("+", 2)
    out_add("-", 2)
    in_y(2)
    in_y(3)
    gather_done("g", G, 3)
    out_partial(3, 0)
    out_partial(3, 1)
    out_zl(1)
    out_x(2)
    out_far("-", 0)
    in_final()
    gather_start("r", RI, RI.at[0, 0, k])
    out_add("+", 3)
    out_pair(1)
    out_add("-", 3)
    out_zl(2)
    gather_y("r", RI, 1, 0, 1)
    gather_y("r", RI, 3, 0, 0)
    gather_y("r", RI, 1, 0, 0)
    gather_y("r", RI, 3, 0, 1)
    out_far("+", 1)
    gather_z("r", RI, 1)
    out_far("-", 1)
    out_pair(2)
    out_x(3)
    gather_far("r", RI, 0)
    gather_z("r", RI, 2)
    gather_y("r", RI, 1, 1, 1)
    gather_y("r", RI, 3, 1, 0)
    out_far("+", 2)
    gather_y("r", RI, 1, 1, 0)
    gather_y("r", RI, 3, 1, 1)
    out_zl(3)
    gather_y("r", RI, 1, 2, 1)
    gather_y("r", RI, 3, 2, 0)
    gather_z("r", RI, 3)
    gather_y("r", RI, 1, 2, 0)
    gather_y("r", RI, 3, 2, 1)
    gather_far("r", RI, 1)
    out_pair(3)
    out_far("+", 3)
    out_far("-", 2)
    gather_far("r", RI, 2)
    gather_y("r", RI, 1, 3, 1)
    gather_y("r", RI, 3, 3, 0)
    coeffs(0)
    out_far("-", 3)
    gather_y("r", RI, 1, 3, 0)
    gather_y("r", RI, 3, 3, 1)
    gather_far("r", RI, 3)
    coeffs(2)
    coeffs(3)
    drain()
    assert (len(sent), len(arrived)) == (SENT, ARRIVED), (len(sent), len(arrived))


def shards(query_grads, query_inputs, out_basis, in_basis, eig_grid):
    bf16, f32, vmem = jnp.bfloat16, jnp.float32, pltpu.VMEM
    any_space = pl.BlockSpec(memory_space=pl.ANY)
    return pl.pallas_call(
        kernel,
        out_shape=jax.ShapeDtypeStruct((896, 1024), bf16),
        in_specs=[any_space] * 5,
        out_specs=any_space,
        scratch_shapes=[
            vmem((4, 4, 2, 32, 3584), bf16),
            vmem((3584, 896), bf16),
            vmem((2, 4, 4, 32, 256), bf16),
            vmem((2, 256, 1024), bf16),
            vmem((4, 4, 32, 1024), bf16),
            vmem((4, 4, 32, 1024), f32),
            vmem((6, 4, 16, 1024), bf16),
            vmem((4, 32, 1024), bf16),
            vmem((32, 1024), f32),
            vmem((3, 32, 1024), bf16),
            vmem((4, 4, 2, 32, 1024), bf16),
            vmem((4, 4, 2, 32, 896), bf16),
            vmem((4, 4, 2, 32, 896), f32),
            vmem((4, 6, 32, 896), bf16),
            vmem((4, 32, 896), bf16),
            vmem((4, 32, 896), bf16),
            vmem((4, 4, 2, 32, 896), bf16),
            vmem((896, 1024), f32),
            vmem((896, 1024), bf16),
            vmem((896, 1024), bf16),
            pltpu.SemaphoreType.DMA((SENT,)),
            pltpu.SemaphoreType.DMA((ARRIVED,)),
            pltpu.SemaphoreType.DMA((9,)),
        ],
        compiler_params=pltpu.CompilerParams(
            collective_id=0, has_side_effects=True, vmem_limit_bytes=56 * 2**20
        ),
        cost_estimate=pl.CostEstimate(flops=9_000_000_000, bytes_accessed=12_000_000, transcendentals=0),
        name="precondition",
    )(query_grads, query_inputs.reshape(4, 4, 2, 32, 256), out_basis, in_basis, eig_grid)


def solution(mesh):
    return jax.shard_map(
        shards,
        mesh=mesh,
        in_specs=(
            P("col", "row"),
            P(None, "col"),
            P("row", "col"),
            P("col", "row"),
            P("col", "row"),
        ),
        out_specs=P("col", "row"),
        check_vma=False,
    )
```

```python
import jax
import jax.numpy as jnp
from jax import lax
from jax.experimental import pallas as pl
from jax.experimental.pallas import tpu as pltpu
from jax.sharding import PartitionSpec as P

damping = 0.01
MESH = pl.DeviceIdType.MESH
SENT, ARRIVED = 12, 101


def kernel(g_in, q_in, bo_in, bi_in, eig_in, out, G, B, QI, IB, RIp, RIf, RZ, JYb, JYf, RY, RI,
           Pb, Pf, RX, SB, SZ, RO, ACC, EIG, SCALE, OUT, ssem, rsem, lsem):
    f32, bf16 = jnp.float32, jnp.bfloat16
    r, c = lax.axis_index("row"), lax.axis_index("col")
    x, zl = r // 2, r % 2
    y, zh, k = c // 8, (c // 2) % 4, c % 2

    def dev(dx=0, dy=0, dz=0, flip_zl=False, flip_k=False):
        zl_to = 1 - zl if flip_zl else zl
        k_to = 1 - k if flip_k else k
        return ((x + dx) % 4 * 2 + zl_to, (y + dy) % 4 * 8 + (zh + dz) % 4 * 2 + k_to)

    sib = dev(flip_k=True)
    yp, ym, y2 = dev(dy=1), dev(dy=3), dev(dy=2)
    zp, zm, z2 = dev(dz=1), dev(dz=3), dev(dz=2)
    xp, xm, x2 = dev(dx=1), dev(dx=3), dev(dx=2)
    zlp = dev(flip_zl=True)
    partners = (sib, yp, ym, y2, zp, zm, z2, xp, xm, x2, zlp)

    loads = {}

    def load(name, src, dst):
        cp = pltpu.make_async_copy(src, dst, lsem.at[len(loads)])
        cp.start()
        loads[name] = cp

    load("q", q_in.at[:, :, k], QI.at[k])
    load("bi", bi_in, IB.at[k])
    load("g", g_in, G.at[0, 0, k])
    load("bo", bo_in, B)
    load("eig", eig_in, EIG)

    barrier = pltpu.get_barrier_semaphore()
    for p in partners:
        pl.semaphore_signal(barrier, inc=1, device_id=p, device_id_type=MESH)
    pl.semaphore_wait(barrier, len(partners))

    sent, arrived = {}, {}

    def copy(group, name, src, dst, to):
        out_sem = ssem.at[sent.setdefault(group, len(sent))]
        in_sem = rsem.at[arrived.setdefault(name, len(arrived))]
        return pltpu.make_async_remote_copy(src_ref=src, dst_ref=dst, send_sem=out_sem, recv_sem=in_sem,
                                            device_id=to, device_id_type=MESH)

    def send(group, name, src, dst, to):
        copy(group, name, src, dst, to).start()

    def got(name, ref):
        copy("ibi", name, ref, ref, sib).wait_recv()

    def all_sent(group, ref):
        copy(group, "ibi", ref, ref, sib).wait_send()

    def part(buf, q, h, dy):
        return buf.at[q, dy, k, pl.ds(16 * h, 16)]

    def send_y(t, buf, q, halves):
        for h in (0, 1):
            send(t + "y", f"{t}y3{q}{h}", halves[h], part(buf, q, h, 3), yp)
            send(t + "y", f"{t}y1{q}{1 - h}", halves[1 - h], part(buf, q, 1 - h, 1), ym)

    def gather_start(t, buf, own):
        halves = [own.at[pl.ds(16 * h, 16)] for h in range(2)]
        send(t + "z", t + "z1", halves[0], part(buf, 1, 0, 0), zp)
        send(t + "z", t + "z1", halves[1], part(buf, 1, 1, 0), zm)
        send(t + "z", t + "z2", halves[1], part(buf, 2, 1, 0), zp)
        send(t + "z", t + "z2", halves[0], part(buf, 2, 0, 0), zm)
        send_y(t, buf, 0, halves)
        send(t + "s", t + "s0", own, buf.at[0, 0, k], sib)

    def gather_z(t, buf, q):
        got(f"{t}z{q}", buf.at[q, 0, k])
        halves = [part(buf, q, h, 0) for h in range(2)]
        if q == 1:
            send(t + "z", t + "z3", halves[0], part(buf, 3, 0, 0), zp)
            send(t + "z", t + "z3", halves[1], part(buf, 3, 1, 0), zm)
        send_y(t, buf, q, halves)
        send(t + "s", f"{t}s{q}", buf.at[q, 0, k], buf.at[q, 0, k], sib)

    def gather_y(t, buf, dy, q, h):
        src = part(buf, q, h, dy)
        got(f"{t}y{dy}{q}{h}", src)
        if (dy, h) == (3, 0):
            send(t + "y", f"{t}y2{q}", src, part(buf, q, 0, 2), yp)
        if (dy, h) == (1, 1):
            send(t + "y", f"{t}y2{q}", src, part(buf, q, 1, 2), ym)
        send(t + "s", f"{t}s{q}", src, src, sib)

    def gather_far(t, buf, q):
        src = buf.at[q, 2, k]
        got(f"{t}y2{q}", src)
        send(t + "s", f"{t}s{q}", src, src, sib)

    def gather_done(t, buf, q):
        got(f"{t}s{q}", buf.at[q, :, 1 - k])

    def in_start():
        send("ibi", "ibi", bi_in, IB.at[k], sib)
        send("iq", "iq", q_in.at[:, :, 1 - k], QI.at[k], sib)

    def in_partial():
        loads["q"].wait()
        loads["bi"].wait()
        got("ibi", IB.at[1 - k])
        got("iq", QI.at[1 - k])
        for yy in range(4):
            total = jnp.zeros((128, 1024), f32)
            for kf in range(2):
                total += jnp.dot(QI[kf, yy].reshape(128, 256), IB[kf], preferred_element_type=f32)
            total = total.reshape(4, 32, 1024)
            for zz in range(4):
                RIf[zz, yy] = total[zz]
                RIp[zz, yy] = total[zz].astype(bf16)

    zn, zb, zo = (zh + 1) % 4, (zh + 3) % 4, (zh + 2) % 4
    lo, hi = pl.ds(0, 16), pl.ds(16, 16)

    def in_far(j):
        yj = (y + j) % 4
        send("i", f"iA+{j}", RIp.at[zo, yj, lo], RZ.at[0, j], zp)
        send("i", f"iA-{j}", RIp.at[zo, yj, hi], RZ.at[1, j], zm)

    def in_near(j):
        yj = (y + j) % 4
        send("i", f"iD{j}", RIp.at[zn, yj, hi], RZ.at[2, j], zp)
        send("i", f"iD{j}", RIp.at[zb, yj, lo], RZ.at[3, j], zm)

    def in_add(way, j):
        got(f"iA{way}{j}", RZ.at[0 if way == "+" else 1, j])
        yj = (y + j) % 4
        if way == "+":
            RIp[zn, yj, lo] = (RIf[zn, yj, lo] + RZ[0, j].astype(f32)).astype(bf16)
            send("i", f"iD{j}", RIp.at[zn, yj, lo], RZ.at[4, j], zp)
        else:
            RIp[zb, yj, hi] = (RIf[zb, yj, hi] + RZ[1, j].astype(f32)).astype(bf16)
            send("i", f"iD{j}", RIp.at[zb, yj, hi], RZ.at[5, j], zm)

    def in_y(j):
        got(f"iD{j}", RZ.at[pl.ds(2, 4), j])
        yj = (y + j) % 4
        first = RIf[zh, yj, lo] + RZ[4, j].astype(f32) + RZ[3, j].astype(f32)
        second = RIf[zh, yj, hi] + RZ[2, j].astype(f32) + RZ[5, j].astype(f32)
        if j == 0:
            JYf[lo] = first
            JYf[hi] = second
        else:
            JYb[j, lo] = first.astype(bf16)
            JYb[j, hi] = second.astype(bf16)
            send("iy", "iy", JYb.at[j], RY.at[j - 1], (yp, y2, ym)[j - 1])

    def in_final():
        got("iy", RY)
        total = JYf[...]
        for i in range(3):
            total += RY[i].astype(f32)
        RI[0, 0, k] = total.astype(bf16)

    xn, xb, xo = (x + 1) % 4, (x + 3) % 4, (x + 2) % 4

    def out_partial(q, n):
        n0, n1 = ((0, 512), (512, 896))[n]
        total = jnp.dot(G[q].reshape(256, 3584), B[:, n0:n1], preferred_element_type=f32)
        total = total.reshape(4, 2, 32, n1 - n0)
        Pf[q, :, :, :, n0:n1] = total
        Pb[q, :, :, :, n0:n1] = total.astype(bf16)
        if n == 1:
            send("x", f"A+{q}", Pb.at[q, xo, 0], RX.at[q, 0], xp)
            send("x", f"A-{q}", Pb.at[q, xo, 1], RX.at[q, 1], xm)
            send("x", f"D{q}", Pb.at[q, xn, 1], RX.at[q, 2], xp)
            send("x", f"D{q}", Pb.at[q, xb, 0], RX.at[q, 3], xm)

    def out_add(way, q):
        got(f"A{way}{q}", RX.at[q, 0 if way == "+" else 1])
        if way == "+":
            Pb[q, xn, 0] = (Pf[q, xn, 0] + RX[q, 0].astype(f32)).astype(bf16)
            send("x", f"D{q}", Pb.at[q, xn, 0], RX.at[q, 4], xp)
        else:
            Pb[q, xb, 1] = (Pf[q, xb, 1] + RX[q, 1].astype(f32)).astype(bf16)
            send("x", f"D{q}", Pb.at[q, xb, 1], RX.at[q, 5], xm)

    def out_x(q):
        got(f"D{q}", RX.at[q, pl.ds(2, 4)])
        Pf[q, x, 0] = Pf[q, x, 0] + RX[q, 4].astype(f32) + RX[q, 3].astype(f32)
        Pf[q, x, 1] = Pf[q, x, 1] + RX[q, 2].astype(f32) + RX[q, 5].astype(f32)
        SB[q] = Pf[q, x, 1 - zl].astype(bf16)
        send("o", f"zl{q}", SB.at[q], SZ.at[q], zlp)

    def out_zl(q):
        got(f"zl{q}", SZ.at[q])
        RO[q, x, zl] = (Pf[q, x, zl] + SZ[q].astype(f32)).astype(bf16)
        mine = RO.at[q, x, zl]
        send("o", f"oz{q}", mine, mine, zlp)
        send("o", f"op{q}", mine, mine, xp)
        send("o", f"o{q}", mine, mine, xm)

    def out_pair(q):
        other = RO.at[q, x, 1 - zl]
        got(f"oz{q}", other)
        send("o", f"o{q}", other, other, xp)
        send("o", f"omz{q}", other, other, xm)

    def out_far(way, q):
        if way == "+":
            src = RO.at[q, xb, zl]
            got(f"op{q}", src)
            send("o", f"o{q}", src, src, xp)
        else:
            src = RO.at[q, xn, 1 - zl]
            got(f"omz{q}", src)
            send("o", f"o{q}", src, src, xm)

    def rotated(q):
        got(f"o{q}", RO.at[q, pl.ds(0, 2)])
        gather_done("r", RI, q)

    def product(left, right):
        return lax.dot_general(left, right, (((0,), (0,)), ((), ())), preferred_element_type=f32)

    outs = []

    def coeffs(q):
        if q == 0:
            rotated(0)
            rotated(1)
            ACC[...] = product(RO[0:2].reshape(512, 896), RI[0:2].reshape(512, 1024))
        elif q == 2:
            rotated(2)
            ACC[...] += product(RO[2].reshape(256, 896), RI[2].reshape(256, 1024))
        else:
            rotated(3)
            right = RI[3].reshape(256, 1024)
            for i, (m, n) in enumerate(((0, 256), (256, 512), (512, 768), (768, 896))):
                total = ACC[m:n] + product(RO[3, :, :, :, m:n].reshape(256, n - m), right)
                OUT[m:n] = (total * SCALE[m:n]).astype(bf16)
                cp = pltpu.make_async_copy(OUT.at[pl.ds(m, n - m)], out.at[pl.ds(m, n - m)], lsem.at[len(loads) + i])
                cp.start()
                outs.append(cp)

    def scale():
        loads["eig"].wait()
        SCALE[...] = 1.0 / (1024 * (EIG[...].astype(f32) + damping))

    def drain():
        for t, buf in (("g", G), ("r", RI)):
            all_sent(t + "z", buf.at[pl.ds(0, 3), 0, 0])
            all_sent(t + "y", buf.at[pl.ds(0, 3), :, 0])
            all_sent(t + "s", buf.at[pl.ds(0, 2)])
        for group, ref in (("ibi", IB.at[k]), ("iq", QI.at[k]), ("i", RZ), ("iy", RY), ("x", RX), ("o", RO)):
            all_sent(group, ref)
        for cp in outs:
            cp.wait()

    gather_start("g", G, g_in)
    in_start()
    in_partial()
    gather_y("g", G, 3, 0, 0)
    gather_y("g", G, 1, 0, 1)
    gather_y("g", G, 1, 0, 0)
    gather_y("g", G, 3, 0, 1)
    in_near(0)
    gather_z("g", G, 1)
    gather_far("g", G, 0)
    loads["g"].wait()
    loads["bo"].wait()
    gather_done("g", G, 0)
    out_partial(0, 0)
    gather_y("g", G, 3, 1, 0)
    gather_y("g", G, 1, 1, 1)
    out_partial(0, 1)
    gather_z("g", G, 2)
    in_far(0)
    in_far(1)
    gather_y("g", G, 1, 1, 0)
    gather_y("g", G, 3, 1, 1)
    in_far(2)
    scale()
    out_add("+", 0)
    out_add("-", 0)
    gather_far("g", G, 1)
    in_far(3)
    in_near(1)
    gather_y("g", G, 3, 2, 0)
    gather_y("g", G, 1, 2, 1)
    gather_done("g", G, 1)
    out_partial(1, 0)
    in_add("+", 0)
    in_add("-", 0)
    gather_z("g", G, 3)
    out_x(0)
    out_partial(1, 1)
    gather_y("g", G, 1, 2, 0)
    gather_y("g", G, 3, 2, 1)
    in_add("+", 1)
    in_add("-", 1)
    in_add("+", 2)
    in_add("-", 2)
    in_add("+", 3)
    gather_far("g", G, 2)
    in_add("-", 3)
    out_add("+", 1)
    out_add("-", 1)
    in_near(2)
    in_near(3)
    gather_y("g", G, 3, 3, 0)
    gather_y("g", G, 1, 3, 1)
    gather_done("g", G, 2)
    out_partial(2, 0)
    in_y(0)
    out_zl(0)
    out_x(1)
    out_partial(2, 1)
    gather_y("g", G, 1, 3, 0)
    gather_y("g", G, 3, 3, 1)
    in_y(1)
    out_far("+", 0)
    out_pair(0)
    gather_far("g", G, 3)
    out_add("+", 2)
    out_add("-", 2)
    in_y(2)
    in_y(3)
    gather_done("g", G, 3)
    out_partial(3, 0)
    out_partial(3, 1)
    out_zl(1)
    out_x(2)
    out_far("-", 0)
    in_final()
    gather_start("r", RI, RI.at[0, 0, k])
    out_add("+", 3)
    out_pair(1)
    out_add("-", 3)
    out_zl(2)
    gather_y("r", RI, 1, 0, 1)
    gather_y("r", RI, 3, 0, 0)
    gather_y("r", RI, 1, 0, 0)
    gather_y("r", RI, 3, 0, 1)
    out_far("+", 1)
    gather_z("r", RI, 1)
    out_far("-", 1)
    out_pair(2)
    out_x(3)
    gather_far("r", RI, 0)
    gather_z("r", RI, 2)
    gather_y("r", RI, 1, 1, 1)
    gather_y("r", RI, 3, 1, 0)
    out_far("+", 2)
    gather_y("r", RI, 1, 1, 0)
    gather_y("r", RI, 3, 1, 1)
    out_zl(3)
    gather_y("r", RI, 1, 2, 1)
    gather_y("r", RI, 3, 2, 0)
    gather_z("r", RI, 3)
    gather_y("r", RI, 1, 2, 0)
    gather_y("r", RI, 3, 2, 1)
    gather_far("r", RI, 1)
    out_pair(3)
    out_far("+", 3)
    out_far("-", 2)
    gather_far("r", RI, 2)
    gather_y("r", RI, 1, 3, 1)
    gather_y("r", RI, 3, 3, 0)
    coeffs(0)
    out_far("-", 3)
    gather_y("r", RI, 1, 3, 0)
    gather_y("r", RI, 3, 3, 1)
    gather_far("r", RI, 3)
    coeffs(2)
    coeffs(3)
    drain()
    assert (len(sent), len(arrived)) == (SENT, ARRIVED), (len(sent), len(arrived))


def shards(query_grads, query_inputs, out_basis, in_basis, eig_grid):
    bf16, f32, vmem = jnp.bfloat16, jnp.float32, pltpu.VMEM
    any_space = pl.BlockSpec(memory_space=pl.ANY)
    return pl.pallas_call(
        kernel,
        out_shape=jax.ShapeDtypeStruct((896, 1024), bf16),
        in_specs=[any_space] * 5,
        out_specs=any_space,
        scratch_shapes=[
            vmem((4, 4, 2, 32, 3584), bf16),
            vmem((3584, 896), bf16),
            vmem((2, 4, 4, 32, 256), bf16),
            vmem((2, 256, 1024), bf16),
            vmem((4, 4, 32, 1024), bf16),
            vmem((4, 4, 32, 1024), f32),
            vmem((6, 4, 16, 1024), bf16),
            vmem((4, 32, 1024), bf16),
            vmem((32, 1024), f32),
            vmem((3, 32, 1024), bf16),
            vmem((4, 4, 2, 32, 1024), bf16),
            vmem((4, 4, 2, 32, 896), bf16),
            vmem((4, 4, 2, 32, 896), f32),
            vmem((4, 6, 32, 896), bf16),
            vmem((4, 32, 896), bf16),
            vmem((4, 32, 896), bf16),
            vmem((4, 4, 2, 32, 896), bf16),
            vmem((896, 1024), f32),
            vmem((896, 1024), bf16),
            vmem((896, 1024), f32),
            vmem((896, 1024), bf16),
            pltpu.SemaphoreType.DMA((SENT,)),
            pltpu.SemaphoreType.DMA((ARRIVED,)),
            pltpu.SemaphoreType.DMA((9,)),
        ],
        compiler_params=pltpu.CompilerParams(
            collective_id=0, has_side_effects=True, vmem_limit_bytes=56 * 2**20
        ),
        cost_estimate=pl.CostEstimate(flops=9_000_000_000, bytes_accessed=12_000_000, transcendentals=0),
        name="precondition",
    )(query_grads, query_inputs.reshape(4, 4, 2, 32, 256), out_basis, in_basis, eig_grid)


def solution(mesh):
    return jax.shard_map(
        shards,
        mesh=mesh,
        in_specs=(
            P("col", "row"),
            P(None, "col"),
            P("row", "col"),
            P("col", "row"),
            P("col", "row"),
        ),
        out_specs=P("col", "row"),
        check_vma=False,
    )
```
